32 devices in a mesh: group: 2 (over y), expert: 4 (over z), tensor: 2 (over x), dp: 2 (over core).
Axes of the slice: x: 2, y: 2, z: 4, core: 2. Of those that a mesh axis runs over, the one named last changes fastest.
Arguments:
- tokens: bfloat16 [2048, 3584], P(('group', 'expert', 'dp')), parts along dimension 0, may hold values from -6 to 6
- norm_gain: float32 [3584], replicated, may hold values from 0.25 to 1.75
- routes: int32 [2048, 2], P(('group', 'expert', 'dp')), parts along dimension 0, may hold values from 0 to 3, all different within a row; in each aligned block of 128 rows (0 to 127, 128 to 255, ...) at most 80 rows name the same one
- gate_values: bfloat16 [2048, 2], P(('group', 'expert', 'dp')), parts along dimension 0, may hold values from 0.19921875 to 1
- dense_gate: bfloat16 [2432, 3584], P(('tensor', 'dp'), 'expert'), may hold values from -0.09375 to 0.09375
- dense_up: bfloat16 [2432, 3584], P(('tensor', 'dp'), 'expert'), may hold values from -0.09375 to 0.09375
- dense_down: bfloat16 [2432, 3584], P(('tensor', 'dp'), 'expert'), may hold values from -0.125 to 0.125
- expert_gate: bfloat16 [4, 2432, 3584], P('expert', ('tensor', 'dp')), may hold values from -0.09375 to 0.09375
- expert_up: bfloat16 [4, 2432, 3584], P('expert', ('tensor', 'dp')), may hold values from -0.09375 to 0.09375
- expert_down: bfloat16 [4, 2432, 3584], P('expert', ('tensor', 'dp')), may hold values from -0.125 to 0.125
Outputs:
- mixed: bfloat16 [2048, 3584], P(('group', 'expert', 'dp'), 'tensor'), parts along dimension 0
The draws below stay inside these ranges and needn't reach their ends.
There are 2 independent parts, one for each index of `group`. The reference program is written for one: setup_inputs(seed, part) draws one part's arguments, and reference() takes and returns one part's arrays. A program takes and returns all parts, laid end to end along the dimension named above; an argument that names none is the same for every part. Nothing has to cross between parts.
Inputs may be any that keep to these rules, and one draw needn't show every extreme that they name: `routes`: in each aligned block of 128 rows no expert is named by more than 80 of the ids, a bound that some block reaches; the 2 ids of a row differ.
All inputs are finite; a program needn't handle non-finite values.
Results may differ from the reference program's by a relative error of at most 0.0095.
Values may be sent and summed in bfloat16 or wider, within the bound.
A program may use at most 128 MiB of HBM per device.

```python
import math
import jax
import jax.numpy as jnp
import numpy as np
from jax import lax

D = 3584
DFF = 2432
EFF = 2432
TOP = 2
TOK_DEV = 128
EXPERTS = 4
CAPD = 80
EBLOCK = 608
TOKENS = 1024


def block_scale(own_key, shape, split, least, top_value):
    loudness, own = 1.0, jax.random.fold_in(own_key, 6)
    for position, blocks in split:
        steps = jnp.exp(jax.random.uniform(jax.random.fold_in(own, position), (blocks,), jnp.float32, least / len(split), top_value / len(split)))
        loudness = loudness * jnp.repeat(steps, shape[position] // blocks).reshape([-1 if axis == position else 1 for axis in range(len(shape))])
    return loudness


def deal_out(key, own, number, rows, count, top, most, skew):
    order = jax.random.permutation(key, count)
    heavy_load, usual = load_shares(count, rows * top, most, skew, True), load_shares(count, rows * top, most, skew, False)
    places = jnp.arange(count)

    def named(tallies, turn):
        used = int((tallies > 0).sum())
        fixed = max(1, used // 4)
        passed = fixed + (places - fixed + turn * (used - fixed)) % max(1, count - fixed)
        return jnp.zeros((count,), jnp.int32).at[order[jnp.where(places < fixed, places, passed)]].set(jnp.asarray(tallies, jnp.int32))

    tallies = jnp.where(number % 4 == 0, named(heavy_load, number // 4), named(usual, number - number // 4 - 1))
    mixed = jax.random.permutation(jax.random.fold_in(own, 3), count)
    giver, taker = mixed[0:count // 2 * 2:2], mixed[1:count // 2 * 2:2]
    slack = jnp.minimum(tallies[giver] - 1, most - tallies[taker]) // 2
    slack = jnp.where((giver == order[0]) | (taker == order[0]) | (tallies[taker] == 0), 0, jnp.maximum(slack, 0))
    passed = jax.random.randint(jax.random.fold_in(own, 4), (count // 2,), 0, 1 << 20) % (slack + 1)
    tallies = tallies.at[giver].add(-passed).at[taker].add(passed)
    items = jnp.searchsorted(jnp.cumsum(tallies), jnp.arange(rows * top), side="right").astype(jnp.int32)
    table = items.reshape(top, rows).T
    table = table[jax.random.permutation(jax.random.fold_in(own, 1), rows)]
    turn = jax.random.randint(jax.random.fold_in(own, 2), (rows, 1), 0, top)
    return jnp.take_along_axis(table, (jnp.arange(top)[None, :] + turn) % top, axis=1)


def load_shares(count, total, limit, lean, full):
    loads = [(1 << 20) // math.isqrt(standing ** lean) + 1 for standing in range(1, count + 1)]
    largest = limit if full else min(limit, max(-(-total // count), total * loads[0] // sum(loads)))
    least = 1 if total - largest >= count - 1 else 0
    counts, surplus = [largest] + [least] * (count - 1), total - largest - least * (count - 1)
    while surplus > 0:
        movable = [i for i in range(1, count) if counts[i] < largest] or [i for i in range(1, count) if counts[i] < limit]
        pool, left = sum([loads[i] for i in movable]), surplus
        for i in movable:
            more = min(limit - counts[i], max(1, left * loads[i] // pool), surplus)
            counts[i] = counts[i] + more
            surplus = surplus - more
    return np.array(counts)


def centred(own_key, extent, deviation, most, shards=(), kind=jnp.bfloat16):
    loudness = block_scale(own_key, extent, shards, -0.22, 0.18) if shards else 1.0
    values = jax.random.normal(own_key, extent, jnp.float32) * deviation * loudness
    return jnp.minimum(jnp.maximum(values, -most), most).astype(kind)


def setup_inputs(seed: int = 0, part: int = 0) -> dict:
    seeds = jax.random.split(jax.random.key(seed), 11)
    own_keys = jax.random.split(jax.random.fold_in(seeds[10], part), 11)
    tokens = centred(own_keys[0], (TOKENS, D), 1.0, 6.0, ((0, 8),))
    norm_gain = jnp.clip(1.0 + 0.15 * jax.random.normal(seeds[1], (D,), jnp.float32), 0.25, 1.75)
    routes_keys = jax.random.split(jax.random.fold_in(own_keys[2], 1), TOKENS // TOK_DEV)
    routes_turns = jax.random.permutation(jax.random.fold_in(own_keys[2], 3), TOKENS // TOK_DEV)
    routes = jax.vmap(lambda own, number: deal_out(jax.random.fold_in(own_keys[2], 2), own, number, TOK_DEV, EXPERTS, TOP, CAPD, 2))(routes_keys, routes_turns).reshape((TOKENS, TOP))
    gate_values = jnp.clip(0.19921875 + 0.80078125 * jax.random.uniform(own_keys[3], (TOKENS, TOP), jnp.float32) ** block_scale(own_keys[3], (TOKENS, TOP), ((0, 8),), -0.2, 0.2), 0.19921875, 1.0).astype(jnp.bfloat16)
    dense_gate = centred(seeds[4], (DFF, D), D ** -0.5, 0.09375, ((0, 4), (1, 4)))
    dense_up = centred(seeds[5], (DFF, D), D ** -0.5, 0.09375, ((0, 4), (1, 4)))
    dense_down = centred(seeds[6], (DFF, D), DFF ** -0.5, 0.125, ((0, 4), (1, 4)))
    expert_gate = centred(seeds[7], (EXPERTS, EFF, D), D ** -0.5, 0.09375, ((0, 4), (1, 4)))
    expert_up = centred(seeds[8], (EXPERTS, EFF, D), D ** -0.5, 0.09375, ((0, 4), (1, 4)))
    expert_down = centred(seeds[9], (EXPERTS, EFF, D), EFF ** -0.5, 0.125, ((0, 4), (1, 4)))
    return dict(tokens=tokens, norm_gain=norm_gain, routes=routes, gate_values=gate_values, dense_gate=dense_gate, dense_up=dense_up, dense_down=dense_down, expert_gate=expert_gate, expert_up=expert_up, expert_down=expert_down)


EPSILON = 1e-05

def root_normed(tokens, norm_gain):
    values = tokens.astype(jnp.float32)
    route_scale_factor = lax.rsqrt(lax.optimization_barrier(jnp.mean(values * values, axis=-1, keepdims=True)) + EPSILON)
    return (values * route_scale_factor * norm_gain).astype(jnp.bfloat16)

def swiglu_rows(inputs, w_gate, w_up):
    dims = (((1,), (1,)), ((), ()))
    gate_part = lax.dot_general(inputs, w_gate, dims, preferred_element_type=jnp.float32)
    up_part = lax.dot_general(inputs, w_up, dims, preferred_element_type=jnp.float32)
    return (jax.nn.silu(gate_part) * up_part).astype(jnp.bfloat16)

def reference(tokens, norm_gain, routes, gate_values, dense_gate, dense_up, dense_down, expert_gate, expert_up, expert_down):
    normed = root_normed(tokens, norm_gain)
    dense_hidden = swiglu_rows(normed, dense_gate, dense_up)
    dense_out = jnp.dot(dense_hidden, dense_down, preferred_element_type=jnp.float32)
    pair_ids = routes.reshape(-1).astype(jnp.int32)
    pair_count = pair_ids.shape[0]
    expert_ids = jnp.arange(EXPERTS, dtype=jnp.int32)
    onehot = (pair_ids[:, None] == expert_ids[None, :]).astype(jnp.int32)
    ranking = lax.optimization_barrier(jnp.sum((jnp.cumsum(onehot, axis=0) - onehot) * onehot, axis=1)).astype(jnp.int32)
    table_size = TOKENS // TOK_DEV * CAPD
    table = jnp.full((EXPERTS, table_size), pair_count, dtype=jnp.int32)
    table = table.at[pair_ids, ranking].set(jnp.arange(pair_count, dtype=jnp.int32))
    padded_rows = jnp.concatenate([normed, jnp.zeros((1, D), normed.dtype)], axis=0)
    blocks = EFF // EBLOCK

    def one_expert(operands):
        index_row, w_gate, w_up, w_down = operands
        token_index = jnp.minimum(index_row // TOP, TOKENS).astype(jnp.int32)
        selected_experts = padded_rows[token_index]
        expert_hidden = swiglu_rows(selected_experts, w_gate, w_up)
        sharded_hidden_state = expert_hidden.reshape(-1, blocks, EBLOCK).astype(jnp.float32)
        sharded_down_weight = w_down.reshape(blocks, EBLOCK, D).astype(jnp.float32)
        layer_block_result = jnp.einsum('lue,uet->lut', sharded_hidden_state, sharded_down_weight).astype(jnp.bfloat16)
        return lax.optimization_barrier(jnp.sum(layer_block_result.astype(jnp.float32), axis=1))
    outputs = lax.map(one_expert, (table, expert_gate, expert_up, expert_down))
    pair_out = jnp.zeros((pair_count + 1, D), jnp.float32)
    pair_out = pair_out.at[table.reshape(-1)].set(outputs.reshape(-1, D))
    expert_out = pair_out[:pair_count].reshape(TOKENS, TOP, D)
    weighted = lax.optimization_barrier(jnp.sum(expert_out * gate_values.astype(jnp.float32)[:, :, None], axis=1))
    return (tokens.astype(jnp.float32) + dense_out + weighted).astype(jnp.bfloat16)
```

```python
import jax
import jax.numpy as jnp
from jax import lax
from jax.sharding import PartitionSpec as P

EPSILON = 1e-05
ROWS = (((1,), (1,)), ((), ()))


def root_normed(tokens, norm_gain):
    values = tokens.astype(jnp.float32)
    scale = lax.rsqrt(jnp.mean(values * values, axis=-1, keepdims=True) + EPSILON)
    return (values * scale * norm_gain).astype(jnp.bfloat16)


def swiglu(inputs, w_gate, w_up):
    gate_part = lax.dot_general(inputs, w_gate, ROWS, preferred_element_type=jnp.float32)
    up_part = lax.dot_general(inputs, w_up, ROWS, preferred_element_type=jnp.float32)
    return jax.nn.silu(gate_part) * up_part


def local(
    tokens,
    norm_gain,
    routes,
    gate_values,
    dense_gate,
    dense_up,
    dense_down,
    expert_gate,
    expert_up,
    expert_down,
):
    tensors = lax.axis_size("tensor")
    experts = lax.axis_size("expert")
    pairs = lax.axis_size("dp")
    tok_rows, features = tokens.shape
    hidden = dense_gate.shape[0]
    share = -(-hidden // experts)
    width = features // tensors
    me = lax.axis_index("expert")

    stacked = jnp.stack([dense_gate, dense_up, dense_down])
    stacked = jnp.pad(stacked, ((0, 0), (0, share * experts - hidden), (0, 0)))
    stacked = stacked.reshape(3, experts, share, -1)
    moved = lax.all_to_all(stacked, "expert", split_axis=1, concat_axis=1, tiled=True)
    moved = moved.transpose(0, 2, 1, 3).reshape(3, share, features)

    normed = root_normed(tokens, norm_gain)
    own_gates = jnp.sum(
        jnp.where(
            routes[:, :, None] == jnp.arange(experts, dtype=jnp.int32),
            gate_values.astype(jnp.float32)[:, :, None],
            0.0,
        ),
        axis=1,
    ).astype(jnp.bfloat16)
    every = lax.all_gather(normed, "expert", axis=0, tiled=False)
    every = lax.all_gather(every, "dp", axis=1, tiled=False).reshape(-1, features)
    gates = lax.all_gather(own_gates, ("expert", "dp"), axis=0, tiled=True)
    gate = lax.dynamic_slice_in_dim(gates, me, 1, 1).astype(jnp.float32)

    expert_hidden = (swiglu(every, expert_gate[0], expert_up[0]) * gate).astype(jnp.bfloat16)
    dense_hidden = swiglu(every, moved[0], moved[1]).astype(jnp.bfloat16)
    combined = jnp.dot(expert_hidden, expert_down[0], preferred_element_type=jnp.float32)
    combined = combined + jnp.dot(dense_hidden, moved[2], preferred_element_type=jnp.float32)

    arranged = (
        combined.astype(jnp.bfloat16)
        .reshape(experts, pairs, tok_rows, tensors, width)
        .transpose(3, 1, 0, 2, 4)
        .reshape(tensors * pairs, experts * tok_rows, width)
    )
    summed = lax.psum_scatter(arranged, ("tensor", "dp"), scatter_dimension=0, tiled=True)[0]
    summed = lax.psum_scatter(summed, "expert", scatter_dimension=0, tiled=True).astype(jnp.float32)
    residual = lax.dynamic_slice_in_dim(tokens, lax.axis_index("tensor") * width, width, 1)
    return (residual.astype(jnp.float32) + summed).astype(jnp.bfloat16)


def solution(mesh):
    placed = (
        P(("group", "expert", "dp"), None),
        P(),
        P(("group", "expert", "dp"), None),
        P(("group", "expert", "dp"), None),
        P(("tensor", "dp"), "expert"),
        P(("tensor", "dp"), "expert"),
        P(("tensor", "dp"), "expert"),
        P("expert", ("tensor", "dp"), None),
        P("expert", ("tensor", "dp"), None),
        P("expert", ("tensor", "dp"), None),
    )
    return jax.shard_map(
        local,
        mesh=mesh,
        in_specs=placed,
        out_specs=P(("group", "expert", "dp"), "tensor"),
        check_vma=False,
    )
```

```python
import functools

import jax
import jax.numpy as jnp
from jax import lax
from jax.experimental import pallas as pl
from jax.experimental.pallas import tpu as pltpu
from jax.sharding import PartitionSpec as P

EPSILON = 1e-05
ROWS = (((1,), (1,)), ((), ()))


def root_normed(tokens, norm_gain):
    values = tokens.astype(jnp.float32)
    scale = lax.rsqrt(jnp.mean(values * values, axis=-1, keepdims=True) + EPSILON)
    return (values * scale * norm_gain).astype(jnp.bfloat16)


def swiglu(inputs, w_gate, w_up):
    gate_part = lax.dot_general(inputs, w_gate, ROWS, preferred_element_type=jnp.float32)
    up_part = lax.dot_general(inputs, w_up, ROWS, preferred_element_type=jnp.float32)
    return jax.nn.silu(gate_part) * up_part


def local_plain(
    tokens,
    norm_gain,
    routes,
    gate_values,
    dense_gate,
    dense_up,
    dense_down,
    expert_gate,
    expert_up,
    expert_down,
):
    tensors = lax.axis_size("tensor")
    experts = lax.axis_size("expert")
    pairs = lax.axis_size("dp")
    tok_rows, features = tokens.shape
    hidden = dense_gate.shape[0]
    share = -(-hidden // experts)
    width = features // tensors
    me = lax.axis_index("expert")

    stacked = jnp.stack([dense_gate, dense_up, dense_down])
    stacked = jnp.pad(stacked, ((0, 0), (0, share * experts - hidden), (0, 0)))
    stacked = stacked.reshape(3, experts, share, -1)
    moved = lax.all_to_all(stacked, "expert", split_axis=1, concat_axis=1, tiled=True)
    moved = moved.transpose(0, 2, 1, 3).reshape(3, share, features)

    normed = root_normed(tokens, norm_gain)
    own_gates = jnp.sum(
        jnp.where(
            routes[:, :, None] == jnp.arange(experts, dtype=jnp.int32),
            gate_values.astype(jnp.float32)[:, :, None],
            0.0,
        ),
        axis=1,
    ).astype(jnp.bfloat16)
    every = lax.all_gather(normed, "expert", axis=0, tiled=False)
    every = lax.all_gather(every, "dp", axis=1, tiled=False).reshape(-1, features)
    gates = lax.all_gather(own_gates, ("expert", "dp"), axis=0, tiled=True)
    gate = lax.dynamic_slice_in_dim(gates, me, 1, 1).astype(jnp.float32)

    expert_hidden = (swiglu(every, expert_gate[0], expert_up[0]) * gate).astype(jnp.bfloat16)
    dense_hidden = swiglu(every, moved[0], moved[1]).astype(jnp.bfloat16)
    combined = jnp.dot(expert_hidden, expert_down[0], preferred_element_type=jnp.float32)
    combined = combined + jnp.dot(dense_hidden, moved[2], preferred_element_type=jnp.float32)

    arranged = (
        combined.astype(jnp.bfloat16)
        .reshape(experts, pairs, tok_rows, tensors, width)
        .transpose(3, 1, 0, 2, 4)
        .reshape(tensors * pairs, experts * tok_rows, width)
    )
    summed = lax.psum_scatter(arranged, ("tensor", "dp"), scatter_dimension=0, tiled=True)[0]
    summed = lax.psum_scatter(summed, "expert", scatter_dimension=0, tiled=True).astype(jnp.float32)
    residual = lax.dynamic_slice_in_dim(tokens, lax.axis_index("tensor") * width, width, 1)
    return (residual.astype(jnp.float32) + summed).astype(jnp.bfloat16)


def meet(partners):
    barrier = pltpu.get_barrier_semaphore()
    for partner in partners:
        pl.semaphore_signal(
            barrier, inc=1, device_id=partner, device_id_type=pl.DeviceIdType.MESH
        )
    pl.semaphore_wait(barrier, len(partners))


def spread_kernel(
    experts, x_ref, g_ref, w_ref, every, gates, moved, loc, zs, zr, gs, gr, ws, wr, xs, xr, ds, dr, ys, yr
):
    group, me = lax.axis_index("group"), lax.axis_index("expert")
    t, d = lax.axis_index("tensor"), lax.axis_index("dp")
    width = x_ref.shape[1] // 2
    part = w_ref.shape[1] // 2
    beside = {"dp": 1 - d}
    across = {"tensor": 1 - t}
    twin = {"group": 1 - group}
    peers = [lax.rem(me + k, experts) for k in range(1, experts)]
    meet([{"expert": e} for e in peers] + [beside, across, twin])

    mine = pl.ds(pl.multiple_of(t * width, 128), width)
    theirs = pl.ds(pl.multiple_of((1 - t) * width, 128), width)
    rows = pl.ds(pl.multiple_of(group * part, 16), part)

    def send(src, dst, to, s, r):
        return pltpu.make_async_remote_copy(
            src_ref=src,
            dst_ref=dst,
            send_sem=s,
            recv_sem=r,
            device_id=to,
            device_id_type=pl.DeviceIdType.MESH,
        )

    started = []
    for k, e in enumerate(peers):
        z = send(x_ref.at[:, mine], every.at[me, d, :, mine], {"expert": e}, zs.at[k], zr.at[k])
        z.start()
        started.append(z)
        z = send(g_ref, gates.at[me, d], {"expert": e}, gs.at[k], gr.at[k])
        z.start()
        started.append(z)
    weights = []
    for k, e in enumerate(peers):
        z = send(w_ref.at[e, rows], moved.at[me, rows], {"expert": e}, ws.at[k], wr.at[k])
        z.start()
        started.append(z)
    n = experts - 1
    own = send(x_ref, every.at[me, d], beside, ds.at[3 * n], dr.at[3 * n])
    own.start()
    own_gates = send(g_ref, gates.at[me, d], beside, ds.at[3 * n + 1], dr.at[3 * n + 1])
    own_gates.start()
    here = [
        pltpu.make_async_copy(x_ref, every.at[me, d], loc.at[0]),
        pltpu.make_async_copy(g_ref, gates.at[me, d], loc.at[1]),
        pltpu.make_async_copy(w_ref.at[me], moved.at[me], loc.at[2]),
    ]
    for c in here:
        c.start()

    sources = [lax.rem(me + experts - k, experts) for k in range(1, experts)]
    passed = []
    for k, e in enumerate(sources):
        block = every.at[e, d, :, mine]
        send(block, block, {"expert": e}, zs.at[k], zr.at[k]).wait_recv()
        c = send(block, block, across, xs.at[k], xr.at[k])
        c.start()
        passed.append(c)
        c = send(block, block, beside, ds.at[k], dr.at[k])
        c.start()
        passed.append(c)
        block = gates.at[e, d]
        send(block, block, {"expert": e}, gs.at[k], gr.at[k]).wait_recv()
        c = send(block, block, beside, ds.at[2 * n + k], dr.at[2 * n + k])
        c.start()
        passed.append(c)
    for k, e in enumerate(sources):
        block = moved.at[e, rows]
        send(block, block, {"expert": e}, ws.at[k], wr.at[k]).wait_recv()
        c = send(block, block, twin, ys.at[k], yr.at[k])
        c.start()
        passed.append(c)
    for k, e in enumerate(sources):
        block = every.at[e, d, :, theirs]
        send(block, block, across, xs.at[k], xr.at[k]).wait_recv()
        c = send(block, block, beside, ds.at[n + k], dr.at[n + k])
        c.start()
        started.append(c)
    other = pl.ds(pl.multiple_of((1 - group) * part, 16), part)
    for k, e in enumerate(sources):
        block = every.at[e, 1 - d, :, mine]
        send(block, block, beside, ds.at[k], dr.at[k]).wait_recv()
        block = every.at[e, 1 - d, :, theirs]
        send(block, block, beside, ds.at[n + k], dr.at[n + k]).wait_recv()
        block = gates.at[e, 1 - d]
        send(block, block, beside, ds.at[2 * n + k], dr.at[2 * n + k]).wait_recv()
        block = moved.at[e, other]
        send(block, block, twin, ys.at[k], yr.at[k]).wait_recv()
    own.wait()
    own_gates.wait()
    for c in here:
        c.wait()
    for c in started + passed:
        c.wait_send()


def spread(experts, x, gates, weights):
    n = experts - 1
    dma = pltpu.SemaphoreType.DMA
    anywhere = pl.BlockSpec(memory_space=pl.ANY)
    return pl.pallas_call(
        functools.partial(spread_kernel, experts),
        out_shape=(
            jax.ShapeDtypeStruct((experts, 2) + x.shape, x.dtype),
            jax.ShapeDtypeStruct((experts, 2) + gates.shape, gates.dtype),
            jax.ShapeDtypeStruct(weights.shape, weights.dtype),
        ),
        in_specs=[anywhere] * 3,
        out_specs=(anywhere,) * 3,
        scratch_shapes=[dma((3,))]
        + [dma((n,))] * 8
        + [dma((3 * n + 2,))] * 2
        + [dma((n,))] * 2,
        compiler_params=pltpu.CompilerParams(
            collective_id=0, has_side_effects=True, vmem_limit_bytes=4 * 1024 * 1024
        ),
        cost_estimate=pl.CostEstimate(flops=0, bytes_accessed=30000000, transcendentals=0),
    )(x, gates, weights)


def layer_kernel(
    experts, tok_ref, every, gates, moved, w_gate, w_up, w_down, out_ref,
    outgoing, kept, from_beside, from_across, zsend, zrecv, ds, dr, xs, xr, zs, zr,
):
    me, t, d = lax.axis_index("expert"), lax.axis_index("tensor"), lax.axis_index("dp")
    beside, across = {"dp": 1 - d}, {"tensor": 1 - t}
    peers = [lax.rem(me + k, experts) for k in range(1, experts)]
    meet([{"expert": e} for e in peers] + [beside, across])

    tok_rows, features = tok_ref.shape
    width = features // 2
    cut = moved.shape[2]
    share = moved.shape[1] // 3
    per_half = width // cut
    f32 = jnp.float32

    def send(src, dst, to, s, r):
        return pltpu.make_async_remote_copy(
            src_ref=src,
            dst_ref=dst,
            send_sem=s,
            recv_sem=r,
            device_id=to,
            device_id_type=pl.DeviceIdType.MESH,
        )

    def by_beside(j):
        return send(outgoing.at[j], from_beside.at[j], beside, ds.at[j], dr.at[j])

    def by_across(j):
        return send(kept.at[j, 1 - t], from_across.at[j], across, xs.at[j], xr.at[j])

    def by_expert(j):
        return send(
            zsend.at[j], zrecv.at[j], {"expert": lax.rem(me + 1 + j, experts)}, zs.at[j], zr.at[j]
        )

    def block_sums(e, b):
        x = every[e, b]
        lanes = gates[e, b].astype(f32)
        column = lax.broadcasted_iota(jnp.int32, lanes.shape, 1)
        gate = jnp.sum(jnp.where(column == me, lanes, 0.0), axis=1, keepdims=True)
        g = lax.dot_general(x, w_gate[0], ROWS, preferred_element_type=f32)
        u = lax.dot_general(x, w_up[0], ROWS, preferred_element_type=f32)
        routed = (g / (1.0 + jnp.exp(-g)) * u * gate).astype(jnp.bfloat16)
        both = jnp.zeros((tok_rows, 2 * share), f32)
        for i in range(experts):
            both += lax.dot_general(
                x[:, i * cut : (i + 1) * cut],
                moved[i, : 2 * share],
                ROWS,
                preferred_element_type=f32,
            )
        g, u = both[:, :share], both[:, share:]
        dense = (g / (1.0 + jnp.exp(-g)) * u).astype(jnp.bfloat16)
        sums = []
        for i in range(experts):
            s = jnp.dot(
                routed, w_down[0, :, i * cut : (i + 1) * cut], preferred_element_type=f32
            )
            s += jnp.dot(dense, moved[i, 2 * share :], preferred_element_type=f32)
            sums.append(s.astype(jnp.bfloat16))
        return sums

    def compute(j):
        e = lax.rem(me + 1 + j, experts)
        for dst, b in ((outgoing, 1 - d), (kept, d)):
            for i, s in enumerate(block_sums(e, b)):
                at = (i % per_half) * cut
                dst[j, i // per_half, :, at : at + cut] = s
            if dst is outgoing:
                by_beside(j).start()

    def join_pair(j):
        by_beside(j).wait_recv()
        kept[j] = (kept[j].astype(f32) + from_beside[j].astype(f32)).astype(jnp.bfloat16)
        by_across(j).start()

    def join_tensor(j):
        by_across(j).wait_recv()
        total = kept[j, t].astype(f32) + from_across[j].astype(f32)
        zsend[j] = total.astype(jnp.bfloat16)

    def turn(j, carry):
        compute(j)

        @pl.when(j >= 1)
        def _():
            join_pair(j - 1)

        @pl.when(j >= 2)
        def _():
            join_tensor(j - 2)
            by_expert(j - 2).start()

        return carry

    lax.fori_loop(0, experts, turn, 0)
    last = experts - 1
    join_pair(last)
    join_tensor(last - 1)
    by_expert(last - 1).start()
    by_across(last).wait_recv()
    own = pl.ds(pl.multiple_of(t * width, 128), width)
    total = kept[last, t].astype(f32) + from_across[last].astype(f32)
    total += tok_ref[:, own].astype(f32)
    for j in range(last):
        by_expert(j).wait_recv()
        total += zrecv[j].astype(f32)
    out_ref[...] = total.astype(out_ref.dtype)
    for j in range(experts):
        by_beside(j).wait_send()
        by_across(j).wait_send()
    for j in range(last):
        by_expert(j).wait_send()


def layer(experts, tokens, every, gates, moved, w_gate, w_up, w_down):
    tok_rows, features = tokens.shape
    width = features // 2
    dma = pltpu.SemaphoreType.DMA
    inside = pl.BlockSpec(memory_space=pltpu.VMEM)
    kind = tokens.dtype
    return pl.pallas_call(
        functools.partial(layer_kernel, experts),
        out_shape=jax.ShapeDtypeStruct((tok_rows, width), kind),
        in_specs=[inside] * 7,
        out_specs=inside,
        scratch_shapes=[
            pltpu.VMEM((experts, 2, tok_rows, width), kind),
            pltpu.VMEM((experts, 2, tok_rows, width), kind),
            pltpu.VMEM((experts, 2, tok_rows, width), kind),
            pltpu.VMEM((experts, tok_rows, width), kind),
            pltpu.VMEM((experts - 1, tok_rows, width), kind),
            pltpu.VMEM((experts - 1, tok_rows, width), kind),
        ]
        + [dma((experts,))] * 4
        + [dma((experts - 1,))] * 2,
        compiler_params=pltpu.CompilerParams(
            collective_id=1, has_side_effects=True, vmem_limit_bytes=56 * 1024 * 1024
        ),
        cost_estimate=pl.CostEstimate(
            flops=17000000000, bytes_accessed=30000000, transcendentals=1000000
        ),
    )(tokens, every, gates, moved, w_gate, w_up, w_down)


def local_kernels(
    tokens,
    norm_gain,
    routes,
    gate_values,
    dense_gate,
    dense_up,
    dense_down,
    expert_gate,
    expert_up,
    expert_down,
):
    experts = lax.axis_size("expert")
    hidden, cut = dense_gate.shape
    share = -(-hidden // (32 * experts)) * 32

    weights = jnp.stack([dense_gate, dense_up, dense_down])
    weights = jnp.pad(weights, ((0, 0), (0, share * experts - hidden), (0, 0)))
    weights = weights.reshape(3, experts, share, cut).transpose(1, 0, 2, 3)
    weights = weights.reshape(experts, 3 * share, cut)
    normed = root_normed(tokens, norm_gain)
    own_gates = jnp.sum(
        jnp.where(
            routes[:, :, None] == jnp.arange(128, dtype=jnp.int32),
            gate_values.astype(jnp.float32)[:, :, None],
            0.0,
        ),
        axis=1,
    ).astype(jnp.bfloat16)
    every, gates, moved = spread(experts, normed, own_gates, weights)
    return layer(experts, tokens, every, gates, moved, expert_gate, expert_up, expert_down)


def solution(mesh):
    placed = (
        P(("group", "expert", "dp"), None),
        P(),
        P(("group", "expert", "dp"), None),
        P(("group", "expert", "dp"), None),
        P(("tensor", "dp"), "expert"),
        P(("tensor", "dp"), "expert"),
        P(("tensor", "dp"), "expert"),
        P("expert", ("tensor", "dp"), None),
        P("expert", ("tensor", "dp"), None),
        P("expert", ("tensor", "dp"), None),
    )
    sizes = dict(mesh.shape)
    paired = sizes["group"] == 2 and sizes["tensor"] == 2 and sizes["dp"] == 2
    return jax.shard_map(
        local_kernels if paired else local_plain,
        mesh=mesh,
        in_specs=placed,
        out_specs=P(("group", "expert", "dp"), "tensor"),
        check_vma=False,
    )
```

```python
import functools

import jax
import jax.numpy as jnp
from jax import lax
from jax.experimental import pallas as pl
from jax.experimental.pallas import tpu as pltpu
from jax.sharding import PartitionSpec as P

EPSILON = 1e-05
ROWS = (((1,), (1,)), ((), ()))


def root_normed(tokens, norm_gain):
    values = tokens.astype(jnp.float32)
    scale = lax.rsqrt(jnp.mean(values * values, axis=-1, keepdims=True) + EPSILON)
    return (values * scale * norm_gain).astype(jnp.bfloat16)


def swiglu(inputs, w_gate, w_up):
    gate_part = lax.dot_general(inputs, w_gate, ROWS, preferred_element_type=jnp.float32)
    up_part = lax.dot_general(inputs, w_up, ROWS, preferred_element_type=jnp.float32)
    return jax.nn.silu(gate_part) * up_part


def local_plain(
    tokens,
    norm_gain,
    routes,
    gate_values,
    dense_gate,
    dense_up,
    dense_down,
    expert_gate,
    expert_up,
    expert_down,
):
    tensors = lax.axis_size("tensor")
    experts = lax.axis_size("expert")
    pairs = lax.axis_size("dp")
    tok_rows, features = tokens.shape
    hidden = dense_gate.shape[0]
    share = -(-hidden // experts)
    width = features // tensors
    me = lax.axis_index("expert")

    stacked = jnp.stack([dense_gate, dense_up, dense_down])
    stacked = jnp.pad(stacked, ((0, 0), (0, share * experts - hidden), (0, 0)))
    stacked = stacked.reshape(3, experts, share, -1)
    moved = lax.all_to_all(stacked, "expert", split_axis=1, concat_axis=1, tiled=True)
    moved = moved.transpose(0, 2, 1, 3).reshape(3, share, features)

    normed = root_normed(tokens, norm_gain)
    own_gates = jnp.sum(
        jnp.where(
            routes[:, :, None] == jnp.arange(experts, dtype=jnp.int32),
            gate_values.astype(jnp.float32)[:, :, None],
            0.0,
        ),
        axis=1,
    ).astype(jnp.bfloat16)
    every = lax.all_gather(normed, "expert", axis=0, tiled=False)
    every = lax.all_gather(every, "dp", axis=1, tiled=False).reshape(-1, features)
    gates = lax.all_gather(own_gates, ("expert", "dp"), axis=0, tiled=True)
    gate = lax.dynamic_slice_in_dim(gates, me, 1, 1).astype(jnp.float32)

    expert_hidden = (swiglu(every, expert_gate[0], expert_up[0]) * gate).astype(jnp.bfloat16)
    dense_hidden = swiglu(every, moved[0], moved[1]).astype(jnp.bfloat16)
    combined = jnp.dot(expert_hidden, expert_down[0], preferred_element_type=jnp.float32)
    combined = combined + jnp.dot(dense_hidden, moved[2], preferred_element_type=jnp.float32)

    arranged = (
        combined.astype(jnp.bfloat16)
        .reshape(experts, pairs, tok_rows, tensors, width)
        .transpose(3, 1, 0, 2, 4)
        .reshape(tensors * pairs, experts * tok_rows, width)
    )
    summed = lax.psum_scatter(arranged, ("tensor", "dp"), scatter_dimension=0, tiled=True)[0]
    summed = lax.psum_scatter(summed, "expert", scatter_dimension=0, tiled=True).astype(jnp.float32)
    residual = lax.dynamic_slice_in_dim(tokens, lax.axis_index("tensor") * width, width, 1)
    return (residual.astype(jnp.float32) + summed).astype(jnp.bfloat16)


def meet(partners):
    barrier = pltpu.get_barrier_semaphore()
    for partner in partners:
        pl.semaphore_signal(
            barrier, inc=1, device_id=partner, device_id_type=pl.DeviceIdType.MESH
        )
    pl.semaphore_wait(barrier, len(partners))


def layer_kernel(
    experts, tok_ref, x_ref, g_ref, w_ref, eg_ref, eu_ref, ed_ref, out_ref,
    every, gates, moved, w_gate, w_up, w_down,
    sums, from_beside, from_across, zsend, zrecv,
    loc, tzs, tzr, gzs, gzr, wzs, wzr, wys, wyr, txs, txr, tds, tdr, os, orr,
    ds, dr, xs, xr, zs, zr,
):
    group, me = lax.axis_index("group"), lax.axis_index("expert")
    t, d = lax.axis_index("tensor"), lax.axis_index("dp")
    beside, across, twin = {"dp": 1 - d}, {"tensor": 1 - t}, {"group": 1 - group}
    meet([{"expert": lax.rem(me + k, experts)} for k in range(1, experts)] + [beside, across, twin])

    tok_rows, features = tok_ref.shape
    width = features // 2
    cut = moved.shape[2]
    share = moved.shape[1] // 3
    part = moved.shape[1] // 2
    per_half = width // cut
    f32 = jnp.float32
    mine = pl.ds(pl.multiple_of(t * width, 128), width)
    theirs = pl.ds(pl.multiple_of((1 - t) * width, 128), width)
    rows = pl.ds(pl.multiple_of(group * part, 16), part)
    other_rows = pl.ds(pl.multiple_of((1 - group) * part, 16), part)

    def send(src, dst, to, s, r):
        return pltpu.make_async_remote_copy(
            src_ref=src,
            dst_ref=dst,
            send_sem=s,
            recv_sem=r,
            device_id=to,
            device_id_type=pl.DeviceIdType.MESH,
        )

    def source(j):
        return lax.rem(me + experts - j, experts)

    def target(j):
        e = lax.rem(me + j, experts)
        return e, {"expert": e}

    def weight_send(j):
        e, to = target(j)
        return send(w_ref.at[e, rows], moved.at[me, rows], to, wzs.at[j], wzr.at[j])

    def weight_twin(j, which):
        block = moved.at[source(j), which]
        return send(block, block, twin, wys.at[j], wyr.at[j])

    def token_send(j):
        e, to = target(j)
        return send(x_ref.at[:, mine], every.at[me, d, :, mine], to, tzs.at[j], tzr.at[j])

    def gate_send(j):
        e, to = target(j)
        return send(g_ref, gates.at[me, d], to, gzs.at[j], gzr.at[j])

    def token_across(j, which):
        block = every.at[source(j), d, :, which]
        return send(block, block, across, txs.at[j], txr.at[j])

    def token_beside(j, b, which, i):
        block = every.at[source(j), b, :, which]
        return send(block, block, beside, tds.at[i, j], tdr.at[i, j])

    def gate_beside(j, b):
        block = gates.at[source(j), b]
        return send(block, block, beside, tds.at[2, j], tdr.at[2, j])

    own = send(x_ref, every.at[me, d], beside, os.at[0], orr.at[0])
    own_gates = send(g_ref, gates.at[me, d], beside, os.at[1], orr.at[1])
    here = [
        pltpu.make_async_copy(w_ref.at[me], moved.at[me], loc.at[0]),
        pltpu.make_async_copy(eg_ref, w_gate, loc.at[1]),
        pltpu.make_async_copy(eu_ref, w_up, loc.at[2]),
        pltpu.make_async_copy(ed_ref, w_down, loc.at[3]),
    ]
    for j in range(1, experts):
        weight_send(j).start()
    own.start()
    own_gates.start()
    for j in range(1, experts):
        gate_send(j).start()
    for c in here:
        c.start()
    every[me, d] = x_ref[...]
    gates[me, d] = g_ref[...]
    for j in range(1, experts):
        weight_send(j).wait_recv()
        weight_twin(j, rows).start()
        token_send(j).start()
    for j in range(1, experts):
        gate_send(j).wait_recv()
        gate_beside(j, d).start()
    for c in here:
        c.wait()
    own.wait()
    own_gates.wait()

    def by_beside(j):
        return send(sums.at[j, 1 - d], from_beside.at[j], beside, ds.at[j], dr.at[j])

    def by_across(j):
        return send(sums.at[j, d, 1 - t], from_across.at[j], across, xs.at[j], xr.at[j])

    def by_expert(j):
        return send(
            zsend.at[j - 1], zrecv.at[j - 1], {"expert": source(j)}, zs.at[j - 1], zr.at[j - 1]
        )

    def fetch(j):
        token_send(j).wait_recv()
        token_across(j, mine).start()
        token_beside(j, d, mine, 0).start()

    def gather(j):
        token_across(j, theirs).wait_recv()
        token_beside(j, d, theirs, 1).start()
        token_beside(j, 1 - d, mine, 0).wait_recv()
        token_beside(j, 1 - d, theirs, 1).wait_recv()

    def compute(j):
        e = source(j)
        both_rows = 2 * tok_rows
        x = every[e].reshape(both_rows, features)
        lanes = gates[e].reshape(both_rows, -1).astype(f32)
        column = lax.broadcasted_iota(jnp.int32, lanes.shape, 1)
        gate = jnp.sum(jnp.where(column == me, lanes, 0.0), axis=1, keepdims=True)
        g = lax.dot_general(x, w_gate[0], ROWS, preferred_element_type=f32)
        u = lax.dot_general(x, w_up[0], ROWS, preferred_element_type=f32)
        routed = (g / (1.0 + jnp.exp(-g)) * u * gate).astype(jnp.bfloat16)
        both = jnp.zeros((both_rows, 2 * share), f32)
        for i in range(experts):
            both += lax.dot_general(
                x[:, i * cut : (i + 1) * cut],
                moved[i, : 2 * share],
                ROWS,
                preferred_element_type=f32,
            )
        g, u = both[:, :share], both[:, share:]
        dense = (g / (1.0 + jnp.exp(-g)) * u).astype(jnp.bfloat16)
        for i in range(experts):
            s = jnp.dot(
                routed, w_down[0, :, i * cut : (i + 1) * cut], preferred_element_type=f32
            )
            s += jnp.dot(dense, moved[i, 2 * share :], preferred_element_type=f32)
            at = (i % per_half) * cut
            sums[j, :, i // per_half, :, at : at + cut] = s.astype(jnp.bfloat16).reshape(
                2, tok_rows, cut
            )
        by_beside(j).start()

    def join_pair(j):
        by_beside(j).wait_recv()
        total = sums[j, d].astype(f32) + from_beside[j].astype(f32)
        sums[j, d] = total.astype(jnp.bfloat16)
        by_across(j).start()

    def join_tensor(j):
        by_across(j).wait_recv()
        total = sums[j, d, t].astype(f32) + from_across[j].astype(f32)
        zsend[j - 1] = total.astype(jnp.bfloat16)
        by_expert(j).start()

    def turn(j, carry):
        @pl.when(j >= 1)
        def _():
            gather(j)

        @pl.when((j >= 1) & (j + 1 < experts))
        def _():
            fetch(j + 1)

        compute(j)

        @pl.when(j >= 2)
        def _():
            join_tensor(j - 1)

        join_pair(j)
        return carry

    fetch(1)
    for j in range(1, experts):
        weight_twin(j, other_rows).wait_recv()
        gate_beside(j, 1 - d).wait_recv()
    lax.fori_loop(0, experts, turn, 0)
    last = experts - 1
    join_tensor(last)
    by_across(0).wait_recv()
    total = sums[0, d, t].astype(f32) + from_across[0].astype(f32)
    total += tok_ref[:, mine].astype(f32)
    for j in range(1, experts):
        by_expert(j).wait_recv()
        total += zrecv[j - 1].astype(f32)
    out_ref[...] = total.astype(out_ref.dtype)
    for j in range(experts):
        by_beside(j).wait_send()
        by_across(j).wait_send()
    for j in range(1, experts):
        by_expert(j).wait_send()
        weight_twin(j, rows).wait_send()
        gate_send(j).wait_send()
        weight_send(j).wait_send()
        gate_beside(j, d).wait_send()
        token_send(j).wait_send()
        token_across(j, mine).wait_send()
        token_beside(j, d, mine, 0).wait_send()
        token_beside(j, d, theirs, 1).wait_send()


def layer(experts, tokens, x, gates, weights, w_gate, w_up, w_down):
    tok_rows, features = tokens.shape
    width = features // 2
    dma = pltpu.SemaphoreType.DMA
    inside = pl.BlockSpec(memory_space=pltpu.VMEM)
    anywhere = pl.BlockSpec(memory_space=pl.ANY)
    kind = tokens.dtype
    return pl.pallas_call(
        functools.partial(layer_kernel, experts),
        out_shape=jax.ShapeDtypeStruct((tok_rows, width), kind),
        in_specs=[inside] * 3 + [anywhere] * 4,
        out_specs=inside,
        scratch_shapes=[
            pltpu.VMEM((experts, 2) + x.shape, kind),
            pltpu.VMEM((experts, 2) + gates.shape, kind),
            pltpu.VMEM(weights.shape, kind),
            pltpu.VMEM(w_gate.shape, kind),
            pltpu.VMEM(w_up.shape, kind),
            pltpu.VMEM(w_down.shape, kind),
            pltpu.VMEM((experts, 2, 2, tok_rows, width), kind),
            pltpu.VMEM((experts, 2, tok_rows, width), kind),
            pltpu.VMEM((experts, tok_rows, width), kind),
            pltpu.VMEM((experts - 1, tok_rows, width), kind),
            pltpu.VMEM((experts - 1, tok_rows, width), kind),
            dma((4,)),
        ]
        + [dma((experts,))] * 10
        + [dma((3, experts))] * 2
        + [dma((2,))] * 2
        + [dma((experts,))] * 6,
        compiler_params=pltpu.CompilerParams(
            collective_id=0, has_side_effects=True, vmem_limit_bytes=56 * 1024 * 1024
        ),
        cost_estimate=pl.CostEstimate(
            flops=17000000000, bytes_accessed=30000000, transcendentals=1000000
        ),
    )(tokens, x, gates, weights, w_gate, w_up, w_down)


def local_kernels(
    tokens,
    norm_gain,
    routes,
    gate_values,
    dense_gate,
    dense_up,
    dense_down,
    expert_gate,
    expert_up,
    expert_down,
):
    experts = lax.axis_size("expert")
    hidden, cut = dense_gate.shape
    share = -(-hidden // (32 * experts)) * 32

    weights = jnp.stack([dense_gate, dense_up, dense_down])
    weights = jnp.pad(weights, ((0, 0), (0, share * experts - hidden), (0, 0)))
    weights = weights.reshape(3, experts, share, cut).transpose(1, 0, 2, 3)
    weights = weights.reshape(experts, 3 * share, cut)
    normed = root_normed(tokens, norm_gain)
    own_gates = jnp.sum(
        jnp.where(
            routes[:, :, None] == jnp.arange(128, dtype=jnp.int32),
            gate_values.astype(jnp.float32)[:, :, None],
            0.0,
        ),
        axis=1,
    ).astype(jnp.bfloat16)
    return layer(
        experts, tokens, normed, own_gates, weights, expert_gate, expert_up, expert_down
    )


def solution(mesh):
    placed = (
        P(("group", "expert", "dp"), None),
        P(),
        P(("group", "expert", "dp"), None),
        P(("group", "expert", "dp"), None),
        P(("tensor", "dp"), "expert"),
        P(("tensor", "dp"), "expert"),
        P(("tensor", "dp"), "expert"),
        P("expert", ("tensor", "dp"), None),
        P("expert", ("tensor", "dp"), None),
        P("expert", ("tensor", "dp"), None),
    )
    sizes = dict(mesh.shape)
    paired = sizes["group"] == 2 and sizes["tensor"] == 2 and sizes["dp"] == 2 and sizes["expert"] >= 3
    return jax.shard_map(
        local_kernels if paired else local_plain,
        mesh=mesh,
        in_specs=placed,
        out_specs=P(("group", "expert", "dp"), "tensor"),
        check_vma=False,
    )
```
